32 devices in a mesh: row: 4 (over x, core), col: 8 (over z, y).
Axes of the slice: x: 2, y: 2, z: 4, core: 2. Of those that a mesh axis runs over, the one named last changes fastest.
Arguments:
- object_slices: bfloat16 [2, 2, 1024, 2048], P(None, None, 'row', 'col'), may hold values from -4 to 4
- probe_wave_parts: float32 [8, 2, 256, 256], P('col'), may hold values from -4 to 4
- prop_phase: float32 [256, 256], replicated, may hold values from -3.140625 to 3.140625
- measured: float32 [128, 256, 256], P(('row', 'col')), may hold values from 0 to 2
- positions: int32 [128, 2], P(('row', 'col')), may hold values from 0 to 255
Outputs:
- grad_object: float32 [2, 2, 1024, 2048], P(None, None, 'row', 'col')
- probe_grad: float32 [8, 2, 256, 256], P('col')
The draws below stay inside these ranges and needn't reach their ends.
Inputs may be any that keep to these rules, and one draw needn't show every extreme that they name: Each device holds only positions inside its own tile; a window covers the tile's rows from its centre row - 128 to centre row + 127, likewise columns.
All inputs are finite; a program needn't handle non-finite values.
Results may differ from the reference program's by a relative error of at most 0.015.
Values may be sent and summed in bfloat16 or wider, within the bound.
No kernel may reach another device: no remote copies, remote signals or barrier semaphores. Data moves between devices by JAX's collectives and lax.ppermute only.
A program may use at most 64 MiB of HBM per device.

```python
import math
import jax
import jax.numpy as jnp
from jax import lax

WIN = 256
SCAN_PER_UNIT = 4
TILE = 256
HALF = 128
ROWS = 1024
COLS = 2048
NPOS = 128
N_ROW = 4
N_COL = 8


def set_ends(entries, rng, low, largest):
    extent = entries.shape
    place = [jax.random.randint(jax.random.fold_in(rng, axis), (), 0, extent[axis]) for axis in range(len(extent))]
    entries = entries.at[tuple(place)].set(low)
    longest = extent.index(max(extent))
    place[longest] = (place[longest] + 1) % extent[longest]
    return entries.at[tuple(place)].set(largest)


def levels(rng, dims, split, smallest, largest):
    gain, own = 1.0, jax.random.fold_in(rng, 6)
    for position, parts in split:
        heights = jnp.exp(jax.random.uniform(jax.random.fold_in(own, position), (parts,), jnp.float32, smallest / len(split), largest / len(split)))
        gain = gain * jnp.repeat(heights, dims[position] // parts).reshape([-1 if axis == position else 1 for axis in range(len(dims))])
    return gain


def noise(rng, extent, spread, bound, shards=(), kind=jnp.bfloat16):
    values = jax.random.normal(rng, extent, jnp.float32) * spread
    if len(shards) > 0:
        values = levels(rng, extent, shards, -0.22, 0.18) * values
    return jnp.clip(values, min=-bound, max=bound).astype(kind)


def setup_inputs(seed: int = 0) -> dict:
    arg_keys = jax.random.split(jax.random.key(seed), 6)
    return {
        "object_slices": noise(arg_keys[0], (2, 2, ROWS, COLS), 0.7, 4.0, ((2, 4), (3, 8))),
        "probe_wave_parts": noise(arg_keys[1], (N_COL, 2, WIN, WIN), 0.7, 4.0, ((0, 8),), jnp.float32),
        "prop_phase": jnp.clip(jax.random.uniform(arg_keys[2], (WIN, WIN), jnp.float32, -3.140625, 3.140625), -3.140625, 3.140625),
        "measured": jnp.clip(2.0 * jax.random.uniform(arg_keys[3], (NPOS, WIN, WIN), jnp.float32) ** levels(arg_keys[3], (NPOS, WIN, WIN), ((0, 32),), -0.2, 0.2), 0.0, 2.0),
        "positions": set_ends(jax.random.randint(arg_keys[4], (NPOS, 2), 0, TILE), jax.random.fold_in(arg_keys[4], 1), 0, TILE - 1).astype(jnp.int32),
    }


def dft_tables(length, direction):
    numbers = jnp.arange(length, dtype=jnp.int32)
    phase_int = numbers[:, None] * numbers[None, :] % length
    angles = 2.0 * math.pi / length * phase_int.astype(jnp.float32)
    cosine = jnp.cos(angles) / math.sqrt(length)
    sine_part = direction * jnp.sin(angles) / math.sqrt(length)
    matrix = jnp.stack([jnp.stack([cosine, sine_part]), jnp.stack([-sine_part, cosine])])
    return matrix.astype(jnp.bfloat16)

def transform(wave_in, matrix):
    matrix32 = matrix.astype(jnp.float32)
    rounded = lax.optimization_barrier(wave_in.astype(jnp.bfloat16)).astype(jnp.float32)
    halfway = jnp.einsum('pqab,nqbc->npac', matrix32, rounded)
    halfway = lax.optimization_barrier(halfway.astype(jnp.bfloat16)).astype(jnp.float32)
    return jnp.einsum('nqac,pqcd->npad', halfway, matrix32)

def complex_mul(former, latter):
    real_part = former[:, 0] * latter[:, 0] - former[:, 1] * latter[:, 1]
    imag_part = former[:, 0] * latter[:, 1] + former[:, 1] * latter[:, 0]
    return jnp.stack([real_part, imag_part], axis=1)

def conj_mul(former, latter):
    real_part = former[:, 0] * latter[:, 0] + former[:, 1] * latter[:, 1]
    imag_part = former[:, 0] * latter[:, 1] - former[:, 1] * latter[:, 0]
    return jnp.stack([real_part, imag_part], axis=1)

def gradient_per_window(extended, window_corners, probe_wave_parts, fresnel_propagator, measured, forward_transform, inverse_transform):
    zero_index = jnp.zeros((), jnp.int32)
    win_size = probe_wave_parts.shape[1]
    windows = jax.vmap(lambda start_pair: lax.dynamic_slice(extended, (zero_index, zero_index, start_pair[0], start_pair[1]), (2, 2, win_size, win_size)))(window_corners)
    windows = windows.astype(jnp.float32)
    slice_one = windows[:, 0]
    slice_two = windows[:, 1]
    first_exit = complex_mul(probe_wave_parts[None], slice_one)
    spectrum = complex_mul(fresnel_propagator[None], transform(first_exit, forward_transform))
    wavefield = transform(spectrum, inverse_transform)
    detector = transform(complex_mul(wavefield, slice_two), forward_transform)
    intensity = detector[:, 0] * detector[:, 0] + detector[:, 1] * detector[:, 1]
    misfit = (intensity - measured)[:, None] * detector
    back_two = transform(misfit, inverse_transform)
    grad_second = conj_mul(wavefield, back_two)
    back_spec = transform(conj_mul(slice_two, back_two), forward_transform)
    back_one = transform(conj_mul(fresnel_propagator[None], back_spec), inverse_transform)
    grad_first = conj_mul(probe_wave_parts[None], back_one)
    probe_sum = lax.optimization_barrier(jnp.sum(conj_mul(slice_one, back_one), axis=0))
    illumination = lax.optimization_barrier(jnp.sum(slice_one[:, 0] * slice_one[:, 0] + slice_one[:, 1] * slice_one[:, 1], axis=0))
    return (jnp.stack([grad_first, grad_second], axis=1), probe_sum, illumination)

def add_windows(total, window_gradient_stack, window_corners):
    zero_index = jnp.zeros((), jnp.int32)
    win_size = window_gradient_stack.shape[-1]

    def place_one(number, current):
        start_pair = window_corners[number]
        where = (zero_index, zero_index, start_pair[0], start_pair[1])
        present = lax.dynamic_slice(current, where, (2, 2, win_size, win_size))
        return lax.dynamic_update_slice(current, present + window_gradient_stack[number], where)
    return lax.fori_loop(0, window_gradient_stack.shape[0], place_one, total)

def reference(object_slices, probe_wave_parts, prop_phase, measured, positions):
    forward_transform = dft_tables(WIN, 1.0)
    inverse_transform = dft_tables(WIN, -1.0)
    padded_object = jnp.pad(object_slices, ((0, 0), (0, 0), (HALF, HALF), (HALF, HALF)))
    fresnel_propagator = jnp.stack([jnp.cos(prop_phase), jnp.sin(prop_phase)])

    def device_step(carry, unit_index):
        grad_pad, probe_sum, illum_sum = carry
        tile_row = unit_index // N_COL
        tile_col = unit_index % N_COL
        local_pos = lax.dynamic_slice_in_dim(positions, (unit_index * SCAN_PER_UNIT).astype(jnp.int32), SCAN_PER_UNIT, 0)
        local_measured_data = lax.dynamic_slice_in_dim(measured, (unit_index * SCAN_PER_UNIT).astype(jnp.int32), SCAN_PER_UNIT, 0)
        offset = jnp.stack([tile_row * TILE, tile_col * TILE]).astype(jnp.int32)
        window_corners = (local_pos + offset[None]).astype(jnp.int32)
        probe_here = lax.dynamic_index_in_dim(probe_wave_parts, tile_col, 0, keepdims=False)
        window_gradient_stack, probe_piece, illumination_piece = gradient_per_window(padded_object, window_corners, probe_here, fresnel_propagator, local_measured_data, forward_transform, inverse_transform)
        grad_pad = add_windows(grad_pad, window_gradient_stack, window_corners)
        probe_now = lax.dynamic_index_in_dim(probe_sum, tile_col, 0, keepdims=False)
        probe_sum = lax.dynamic_update_index_in_dim(probe_sum, probe_now + probe_piece, tile_col, 0)
        illum_now = lax.dynamic_index_in_dim(illum_sum, tile_col, 0, keepdims=False)
        illum_sum = lax.dynamic_update_index_in_dim(illum_sum, illum_now + illumination_piece, tile_col, 0)
        return ((grad_pad, probe_sum, illum_sum), None)
    initial = (jnp.zeros(padded_object.shape, jnp.float32), jnp.zeros((N_COL, 2, WIN, WIN), jnp.float32), jnp.zeros((N_COL, WIN, WIN), jnp.float32))
    (grad_pad, probe_sum, illum_sum), _ = lax.scan(device_step, initial, jnp.arange(N_ROW * N_COL, dtype=jnp.int32))
    grad_object = grad_pad[:, :, HALF:HALF + ROWS, HALF:HALF + COLS]
    probe_grad = probe_sum / jnp.sqrt(illum_sum + 1e-06)[:, None]
    return (grad_object, probe_grad)
```

```python
import math

import jax
import jax.numpy as jnp
import ml_dtypes
import numpy as np
from jax import lax
from jax.experimental import pallas as pl
from jax.experimental.pallas import tpu as pltpu
from jax.sharding import PartitionSpec as P

LANES = 128
BF16 = jnp.bfloat16
F32 = jnp.float32


def dft_tables(length):
    numbers = np.arange(length)
    phase_int = numbers[:, None] * numbers[None, :] % length
    angles = np.float32(2.0 * math.pi / length) * phase_int.astype(np.float32)
    scale = np.float32(math.sqrt(length))
    cosine = np.cos(angles) / scale
    sine = np.sin(angles) / scale
    one = np.block([[cosine, sine], [-sine, cosine]])
    other = np.block([[cosine, -sine], [sine, cosine]])
    return one.astype(ml_dtypes.bfloat16), other.astype(ml_dtypes.bfloat16)


def mul(a, b):
    return a[0] * b[0] - a[1] * b[1], a[0] * b[1] + a[1] * b[0]


def conj_mul(a, b):
    return a[0] * b[0] + a[1] * b[1], a[0] * b[1] - a[1] * b[0]


def pairs(axis, odd):
    swaps = []
    for i in range(odd, lax.axis_size(axis) - 1, 2):
        swaps += [(i, i + 1), (i + 1, i)]
    return swaps


def swap(x, axis, odd):
    return lax.ppermute(x, axis, pairs(axis, odd))


def edge(x, dim, width, parity):
    return lax.dynamic_slice_in_dim(x, parity * (x.shape[dim] - width), width, dim)


def chain_kernel(
    place, positions, center, col_even, col_odd, row_even, row_odd, probe, prop, meas, one, other,
    own, sides, send_even, send_odd, probe_sum, illumination, ext, acc, wave,
):
    n = pl.program_id(0)
    win = probe.shape[1]
    half = win // 2
    tiles = 2 * win // LANES
    row_parity, col_parity = place[0], place[1]

    def lanes(t):
        return slice(t * LANES, (t + 1) * LANES)

    @pl.when(n == 0)
    def assemble():
        for p in range(4):
            a, b = p // 2, p % 2
            for t in range(tiles):
                low = t * LANES
                if half <= low < half + win:
                    ext[p, t, half : half + win, :] = center[a, b, :, lanes(t - half // LANES)].astype(F32)

        def put_cols(before, after):
            for p in range(4):
                a, b = p // 2, p % 2
                for t in range(half // LANES):
                    ext[p, t, half : half + win, :] = before[a, b, :, lanes(t)].astype(F32)
                    late = (half + win) // LANES + t
                    ext[p, late, half : half + win, :] = after[a, b, :, lanes(t)].astype(F32)

        def put_rows(before, after):
            for p in range(4):
                a, b = p // 2, p % 2
                for t in range(tiles):
                    ext[p, t, :half, :] = before[a, b, :, lanes(t)].astype(F32)
                    ext[p, t, half + win :, :] = after[a, b, :, lanes(t)].astype(F32)

        pl.when(col_parity == 0)(lambda: put_cols(col_odd, col_even))
        pl.when(col_parity == 1)(lambda: put_cols(col_even, col_odd))
        pl.when(row_parity == 0)(lambda: put_rows(row_odd, row_even))
        pl.when(row_parity == 1)(lambda: put_rows(row_even, row_odd))
        acc[...] = jnp.zeros_like(acc)
        probe_sum[...] = jnp.zeros_like(probe_sum)
        illumination[...] = jnp.zeros_like(illumination)

    row, col = positions[n, 0], positions[n, 1]
    tile = col // LANES
    shift = col - tile * LANES
    lane = lax.broadcasted_iota(jnp.int32, (win, LANES), 1)
    count = win // LANES

    def window(p):
        back = lax.rem(LANES - shift, LANES)
        parts = [pltpu.roll(ext[p, tile + j, pl.ds(row, win), :], back, 1) for j in range(count + 1)]
        keep = lane < LANES - shift
        return jnp.concatenate([jnp.where(keep, parts[j], parts[j + 1]) for j in range(count)], axis=1)

    def add_window(p, value):
        parts = [pltpu.roll(value[:, lanes(j)], shift, 1) for j in range(count)]
        keep = lane >= shift
        for j in range(count + 1):
            left = parts[j - 1] if j > 0 else 0.0
            right = parts[j] if j < count else 0.0
            acc[p, tile + j, pl.ds(row, win), :] += jnp.where(keep, right, left)

    def transform(u, left, right):
        stacked = jnp.concatenate([u[0].astype(BF16), u[1].astype(BF16)], axis=0)
        halfway = jnp.dot(left[...], stacked, preferred_element_type=F32).astype(BF16)
        halfway = jnp.concatenate([halfway[:win], halfway[win:]], axis=1)
        result = jnp.dot(halfway, right[...], preferred_element_type=F32)
        return result[:, :win], result[:, win:]

    def forward(u):
        return transform(u, one, other)

    def inverse(u):
        return transform(u, other, one)

    def whole(ref):
        return ref[0], ref[1]

    spectrum = mul(whole(prop), forward(mul(whole(probe), (window(0), window(1)))))
    wavefield = inverse(spectrum)
    wave[0] = wavefield[0]
    wave[1] = wavefield[1]
    detector = forward(mul(wavefield, (window(2), window(3))))
    residual = detector[0] * detector[0] + detector[1] * detector[1] - meas[0]
    back_two = inverse((residual * detector[0], residual * detector[1]))
    grad_second = conj_mul(whole(wave), back_two)
    add_window(2, grad_second[0])
    add_window(3, grad_second[1])
    back_spec = forward(conj_mul((window(2), window(3)), back_two))
    back_one = inverse(conj_mul(whole(prop), back_spec))
    grad_first = conj_mul(whole(probe), back_one)
    add_window(0, grad_first[0])
    add_window(1, grad_first[1])
    slice_one = (window(0), window(1))
    part = conj_mul(slice_one, back_one)
    probe_sum[0] += part[0]
    probe_sum[1] += part[1]
    illumination[...] += slice_one[0] * slice_one[0] + slice_one[1] * slice_one[1]

    @pl.when(n == pl.num_programs(0) - 1)
    def finish():
        def put_rows(before, after):
            for p in range(4):
                a, b = p // 2, p % 2
                for t in range(tiles):
                    before[a, b, :, lanes(t)] = acc[p, t, :half, :].astype(BF16)
                    after[a, b, :, lanes(t)] = acc[p, t, half + win :, :].astype(BF16)

        pl.when(row_parity == 0)(lambda: put_rows(send_odd, send_even))
        pl.when(row_parity == 1)(lambda: put_rows(send_even, send_odd))
        for p in range(4):
            a, b = p // 2, p % 2
            for t in range(tiles):
                low = t * LANES
                rows = acc[p, t, half : half + win, :]
                if half <= low < half + win:
                    own[a, b, :, lanes(t - half // LANES)] = rows
                elif low < half:
                    sides[a, b, :, lanes(t)] = rows
                else:
                    sides[a, b, :, lanes(t - win // LANES)] = rows


def full(shape):
    return pl.BlockSpec(tuple(shape), lambda *_: (0,) * len(shape))


def chain(place, positions, center, cols, rows, probe, prop, measured):
    win = probe.shape[1]
    half = win // 2
    tables = [jnp.asarray(t) for t in dft_tables(win)]
    args = (center, *cols, *rows, probe, prop, measured, *tables)
    in_specs = [full(x.shape) for x in args]
    in_specs[7] = pl.BlockSpec((1, win, win), lambda n, *_: (n, 0, 0))
    outs = [
        jax.ShapeDtypeStruct((2, 2, win, win), F32),
        jax.ShapeDtypeStruct((2, 2, win, win), F32),
        jax.ShapeDtypeStruct((2, 2, half, 2 * win), BF16),
        jax.ShapeDtypeStruct((2, 2, half, 2 * win), BF16),
        jax.ShapeDtypeStruct((2, win, win), F32),
        jax.ShapeDtypeStruct((win, win), F32),
    ]
    grid = pltpu.PrefetchScalarGridSpec(
        num_scalar_prefetch=2,
        grid=(positions.shape[0],),
        in_specs=in_specs,
        out_specs=[full(o.shape) for o in outs],
        scratch_shapes=[
            pltpu.VMEM((4, 2 * win // LANES, 2 * win, LANES), F32),
            pltpu.VMEM((4, 2 * win // LANES, 2 * win, LANES), F32),
            pltpu.VMEM((2, win, win), F32),
        ],
    )
    return pl.pallas_call(
        chain_kernel,
        out_shape=outs,
        grid_spec=grid,
        compiler_params=pltpu.CompilerParams(vmem_limit_bytes=56 * 1024 * 1024),
        name="chain",
    )(place, positions, *args)


def sides_kernel(place, sides, row_even, row_odd, send_even, send_odd):
    win = sides.shape[2]
    half = win // 2

    def put(before, after, row_before, row_after):
        for a in range(2):
            for b in range(2):
                for out, low, far in ((before, 0, 0), (after, half, win + half)):
                    here = slice(low, low + half)
                    there = slice(far, far + half)
                    out[a, b, :half] = (sides[a, b, :half, here] + row_before[a, b, :, there].astype(F32)).astype(BF16)
                    out[a, b, half:] = (sides[a, b, half:, here] + row_after[a, b, :, there].astype(F32)).astype(BF16)

    for rp in range(2):
        for cp in range(2):
            rows = (row_even, row_odd) if rp else (row_odd, row_even)
            cols = (send_even, send_odd) if cp else (send_odd, send_even)
            pl.when((place[0] == rp) & (place[1] == cp))(lambda cols=cols, rows=rows: put(*cols, *rows))


def fold_sides(place, sides, rows):
    win = sides.shape[2]
    outs = [jax.ShapeDtypeStruct((2, 2, win, win // 2), BF16)] * 2
    return pl.pallas_call(
        sides_kernel,
        out_shape=outs,
        grid_spec=pltpu.PrefetchScalarGridSpec(
            num_scalar_prefetch=1,
            grid=(1,),
            in_specs=[full(x.shape) for x in (sides, *rows)],
            out_specs=[full(o.shape) for o in outs],
        ),
        name="sides",
    )(place, sides, *rows)


def total_kernel(place, own, row_even, row_odd, col_even, col_odd, out):
    win = own.shape[2]
    half = win // 2

    def put(row_before, row_after, col_before, col_after):
        for a in range(2):
            for b in range(2):
                for low, cols in ((0, col_before), (half, col_after)):
                    here = slice(low, low + half)
                    there = slice(half + low, 2 * half + low)
                    for top, rows in ((0, row_before), (half, row_after)):
                        down = slice(top, top + half)
                        out[a, b, down, here] = (
                            own[a, b, down, here]
                            + rows[a, b, :, there].astype(F32)
                            + cols[a, b, down, :].astype(F32)
                        )

    for rp in range(2):
        for cp in range(2):
            rows = (row_even, row_odd) if rp else (row_odd, row_even)
            cols = (col_even, col_odd) if cp else (col_odd, col_even)
            pl.when((place[0] == rp) & (place[1] == cp))(lambda cols=cols, rows=rows: put(*rows, *cols))


def fold_total(place, own, rows, cols):
    return pl.pallas_call(
        total_kernel,
        out_shape=jax.ShapeDtypeStruct(own.shape, F32),
        grid_spec=pltpu.PrefetchScalarGridSpec(
            num_scalar_prefetch=1,
            grid=(1,),
            in_specs=[full(x.shape) for x in (own, *rows, *cols)],
            out_specs=full(own.shape),
        ),
        name="total",
    )(place, own, *rows, *cols)


def on_device(object_slices, probe_wave_parts, prop_phase, measured, positions):
    probe = probe_wave_parts[0]
    half = probe.shape[1] // 2
    row_parity = lax.axis_index("row") % 2
    col_parity = lax.axis_index("col") % 2
    place = jnp.stack([row_parity, col_parity]).astype(jnp.int32)

    cols = (
        swap(edge(object_slices, 3, half, 1 - col_parity), "col", 0),
        swap(edge(object_slices, 3, half, col_parity), "col", 1),
    )
    before = jnp.where(col_parity == 0, cols[1], cols[0])
    after = jnp.where(col_parity == 0, cols[0], cols[1])
    wide = jnp.concatenate([before, object_slices, after], axis=3)
    rows = (
        swap(edge(wide, 2, half, 1 - row_parity), "row", 0),
        swap(edge(wide, 2, half, row_parity), "row", 1),
    )
    prop = jnp.stack([jnp.cos(prop_phase), jnp.sin(prop_phase)])
    own, sides, row_even, row_odd, probe_sum, illumination = chain(
        place, positions, object_slices, cols, rows, probe, prop, measured
    )
    got_rows = (swap(row_even, "row", 0), swap(row_odd, "row", 1))
    col_even, col_odd = fold_sides(place, sides, got_rows)
    got_cols = (swap(col_even, "col", 0), swap(col_odd, "col", 1))
    grad_object = fold_total(place, own, got_rows, got_cols)
    totals = lax.psum((probe_sum, illumination), "row")
    probe_grad = totals[0] / jnp.sqrt(totals[1] + 1e-06)[None]
    return (grad_object, probe_grad[None])


def solution(mesh):
    return jax.shard_map(
        on_device,
        mesh=mesh,
        in_specs=(
            P(None, None, "row", "col"),
            P("col", None, None, None),
            P(),
            P(("row", "col"), None, None),
            P(("row", "col"), None),
        ),
        out_specs=(P(None, None, "row", "col"), P("col", None, None, None)),
        check_vma=False,
    )
```
